256 devices in a mesh: tm: 16 (over y, z_lo, core), space: 16 (over x, z_hi).
Axes of the slice: x: 4, y: 4, z: 8 (z_hi: 4, z_lo: 2; z = z_hi * 2 + z_lo), core: 2. Of those that a mesh axis runs over, the one named last changes fastest.
Arguments:
- initial: float32 [2, 32, 128, 128], P(None, 'space'), may hold values from 0 to 1
- estimate: float32 [16, 2, 32, 128, 128], P('tm', None, 'space'), may hold values from 0 to 1, as said below
- feed_rate: float32 [32, 128, 128], P('space'), may hold values from 0.01 to 0.08
- kill_rate: float32 [32, 128, 128], P('space'), may hold values from 0.02 to 0.07
Outputs:
- corrected: float32 [16, 2, 32, 128, 128], P('tm', None, 'space')
- residual: float32 [16, 2, 32, 128, 128], P('tm', None, 'space')
The draws below stay inside these ranges and needn't reach their ends.
Inputs may be any that keep to these rules, and one draw needn't show every extreme that they name: `estimate`: substrate and catalyst values.
All inputs are finite; a program needn't handle non-finite values.
Results may differ from the reference program's by a relative error of at most 0.00002.
Values sent between devices are 32-bit elements; how exact they have to be, the bound alone decides.
A program may use at most 64 MiB of HBM per device.

```python
import math
import jax
import jax.numpy as jnp
from jax import lax

FACTOR = 4
NT = 16
NZ = 32
NX = 128
NY = 128


def draw_initial(key, part):
    key = jax.random.fold_in(key, 1)
    key_sub, key_cat = jax.random.split(key)
    shape = (NZ, NX, NY)
    substrate = jax.random.uniform(key_sub, shape, jnp.float32, 0.4, 1.0)
    catalyst = jax.random.uniform(key_cat, shape, jnp.float32, 0.0, 0.5)
    return jnp.stack([substrate, catalyst]).astype(jnp.float32)


def draw_estimate(key, part):
    key = jax.random.fold_in(key, 2)
    key_sub, key_cat = jax.random.split(key)
    shape = (NT, NZ, NX, NY)
    substrate = jax.random.uniform(key_sub, shape, jnp.float32, 0.4, 1.0)
    catalyst = jax.random.uniform(key_cat, shape, jnp.float32, 0.0, 0.5)
    return jnp.stack([substrate, catalyst], axis=1).astype(jnp.float32)


def shard_levels(rng, shape, pieces, low, high):
    gain, own = 1.0, jax.random.fold_in(rng, 6)
    for position, shards_of in pieces:
        steps = jnp.exp(jax.random.uniform(jax.random.fold_in(own, position), (shards_of,), jnp.float32, low / len(pieces), high / len(pieces)))
        gain = gain * jnp.repeat(steps, shape[position] // shards_of).reshape([-1 if axis == position else 1 for axis in range(len(shape))])
    return gain


def setup_inputs(seed: int = 0) -> dict:
    seeds = jax.random.split(jax.random.key(seed), 5)
    return {
        "initial": draw_initial(jax.random.fold_in(seeds[4], 71), 0),
        "estimate": draw_estimate(jax.random.fold_in(seeds[4], 71), 0),
        "feed_rate": jnp.clip(jnp.exp(math.log(0.08) - 2.0794415 * jax.random.uniform(seeds[2], (NZ, NX, NY), jnp.float32) ** shard_levels(seeds[2], (NZ, NX, NY), ((0, 16),), -0.2, 0.2)), 0.01, 0.08),
        "kill_rate": jnp.clip(jnp.exp(math.log(0.07) - 1.252763 * jax.random.uniform(seeds[3], (NZ, NX, NY), jnp.float32) ** shard_levels(seeds[3], (NZ, NX, NY), ((0, 16),), -0.2, 0.2)), 0.02, 0.07),
    }


time_step = 0.25
diffusion_substrate = 0.16
diffusion_catalyst = 0.08


def advance(extended, coefficients, step_size):
    middle = extended[..., 1:-1, :, :]
    neighbours = extended[..., 2:, :, :] + extended[..., :-2, :, :]
    neighbours = neighbours + jnp.roll(middle, 1, -2) + jnp.roll(middle, -1, -2)
    neighbours = neighbours + jnp.roll(middle, 1, -1) + jnp.roll(middle, -1, -1)
    laplace = neighbours - 6.0 * middle
    substrate = middle[..., 0, :, :, :]
    catalyst = middle[..., 1, :, :, :]
    reaction = substrate * catalyst * catalyst
    feeding = coefficients[0]
    killing = coefficients[1]
    new_substrate = substrate + step_size * (diffusion_substrate * laplace[..., 0, :, :, :] - reaction + feeding * (1.0 - substrate))
    new_catalyst = catalyst + step_size * (diffusion_catalyst * laplace[..., 1, :, :, :] + reaction - (feeding + killing) * catalyst)
    return jnp.stack([new_substrate, new_catalyst], axis=-4)


def wrap_planes(field):
    return jnp.concatenate([field[..., -1:, :, :], field, field[..., :1, :, :]], axis=-3)


def reference(initial, estimate, feed_rate, kill_rate):
    coefficients = jnp.stack([feed_rate, kill_rate])

    def fine_step(field):
        return advance(wrap_planes(field), coefficients, time_step)

    def coarse_step(field):
        return advance(wrap_planes(field), coefficients, time_step * FACTOR)

    def start_of(ends):
        return jnp.concatenate([initial[None], ends[:-1]], axis=0)

    def relax_points(field):
        for count in range(FACTOR - 1):
            field = fine_step(field)
        return field

    first = start_of(estimate)
    ends = fine_step(relax_points(first))
    second = start_of(ends)
    fine_end = fine_step(relax_points(second))
    residual = fine_end - ends
    defect = fine_end - coarse_step(second)

    def link(coarse_value, term):
        coarse_value = coarse_step(coarse_value) + term
        return coarse_value, coarse_value

    unused, corrected = lax.scan(link, initial, defect)
    return corrected, residual
```

```python
import jax
import jax.numpy as jnp
from jax import lax
from jax.experimental import pallas as pl
from jax.experimental.pallas import tpu as pltpu
from jax.sharding import PartitionSpec as P

FACTOR = 4
time_step = 0.25
diffusion_substrate = 0.16
diffusion_catalyst = 0.08

MESH = pl.DeviceIdType.MESH
F32 = jnp.float32

STATE, COEF, ENDS, START, DEFECT, MIDDLE, TRAIL = 0, 4, 5, 9, 10, 17, 18
FIELDS = 24
SLOTS = 4
LAST_PACK = 18


def place(x, r, group):
    snake = r < 12
    y = jnp.where(snake, lax.div(r, 3), 15 - r)
    t = lax.rem(r, 3)
    q = jnp.where(snake, jnp.where(lax.rem(y, 2) == 0, 1 + t, 3 - t), 0)
    z = 4 * lax.div(group, 2) + q
    core = 1 - lax.rem(group, 2)
    return y * 4 + lax.rem(z, 2) * 2 + core, x * 4 + lax.div(z, 2)


def roll(value, by, axis):
    return pltpu.roll(value, by % value.shape[axis], axis)


def kernel(
    initial, estimate, feed, kill, corrected, residual,
    field, land, pack, coef, work, late, coarse, back, diff, zero,
    halo_in, halo_out, block_in, block_out, first_out, coef_out, diff_out, corr_out,
    diff_in, corr_in, back_in, back_out, zero_sem,
):
    tm = lax.axis_index("tm")
    space = lax.axis_index("space")
    x, z_hi = lax.div(space, 4), lax.rem(space, 4)
    y, z_lo, core = lax.div(tm, 4), lax.rem(lax.div(tm, 2), 2), lax.rem(tm, 2)
    z = 2 * z_hi + z_lo
    cube, q = lax.div(z, 4), lax.rem(z, 4)
    r = jnp.where(q == 0, 15 - y, 3 * y + jnp.where(lax.rem(y, 2) == 0, q - 1, 3 - q))
    group = 2 * cube + 1 - core
    x_up, x_down = lax.rem(x + 1, 4), lax.rem(x + 3, 4)
    r_up, r_down = lax.rem(r + 1, 16), lax.rem(r + 15, 16)

    barrier = pltpu.get_barrier_semaphore()

    def greet(target):
        pl.semaphore_signal(barrier, inc=1, device_id=target, device_id_type=MESH)

    me = tm * 4 + z_hi

    @pl.loop(1, 64)
    def _(i):
        other = lax.rem(me + i, 64)
        greet((lax.div(other, 4), x * 4 + lax.rem(other, 4)))

    for side in (x_up, x_down):
        for row in (r_down, r, r_up):
            for other in range(4):
                greet(place(side, row, other))
    pl.semaphore_wait(barrier, 63 + 24)

    def is_me(target):
        return jnp.logical_and(target[0] == tm, target[1] == space)

    def put(src, dst, out_sem, in_sem, target):
        same = is_me(target)

        @pl.when(same)
        def _():
            pltpu.make_async_copy(src, dst, in_sem).start()

        @pl.when(jnp.logical_not(same))
        def _():
            pltpu.make_async_remote_copy(src, dst, out_sem, in_sem, device_id=target, device_id_type=MESH).start()

    def put_done(src, out_sem, target):
        @pl.when(jnp.logical_not(is_me(target)))
        def _():
            pltpu.make_async_copy(src, src, out_sem).wait()

    def rows_of(row):
        return pl.ds(pl.multiple_of(row * 8, 8), 8)

    here = pl.ds(4 + 2 * z_hi, 2)
    turn = lax.rem(tm + 1, 16)
    slot_there, group_there = lax.rem(turn, 4), lax.div(turn, 4)
    coef_row = jnp.where(lax.rem(tm, 4) == 0, 15 - y, 3 * y + jnp.where(lax.rem(y, 2) == 0, lax.rem(tm, 4) - 1, 3 - lax.rem(tm, 4)))

    def coef_put(other):
        target = place(x, coef_row, other)
        for k, src in enumerate((feed, kill)):
            put(src.at[:, rows_of(coef_row), :], field.at[COEF, k, here, 0:8, :], coef_out.at[other, k], block_in.at[COEF], target)

    for other in range(4):
        coef_put(other)

    def first_put(src):
        @pl.loop(0, 16)
        def _(i):
            row = lax.rem(r + i, 16)
            put(
                src.at[:, :, rows_of(row), :], field.at[slot_there, :, here, 0:8, :],
                first_out.at[i], block_in.at[slot_there], place(x, row, group_there),
            )

    @pl.when(tm < 15)
    def _():
        first_put(estimate.at[0])

    @pl.when(tm == 15)
    def _():
        first_put(initial)

    @pl.when(tm == 0)
    def _():
        zero[...] = jnp.zeros_like(zero)
        pltpu.make_async_copy(zero, residual.at[0], zero_sem).start()

    low = lax.broadcasted_iota(jnp.int32, (8, 128), 0)
    half = low < 4

    def block_of(f):
        return field.at[f, :, 4:12, 0:8, :]

    def send_halo(f, p, there, target_group):
        for k in range(2):
            plane = [field[f, k, 4 + b, 0:8, :] for b in range(8)]
            for t in range(4):
                a, b = plane[2 * t], plane[2 * t + 1]
                pack[p, 0, k, t] = jnp.where(half, a, roll(b, 4, 0))
                pack[p, 1, k, t] = jnp.where(half, roll(a, 4, 0), b)
            for side, near in ((0, (7, 6, 5)), (1, (0, 1, 2))):
                a, b, c = (plane[n] for n in near)
                pack[p, 2, k, 2 * side] = jnp.where(low < 3, a, jnp.where(low < 5, roll(b, 3, 0), roll(c, 5, 0)))
                pack[p, 2, k, 2 * side + 1] = jnp.where(low >= 5, a, jnp.where(low >= 3, roll(b, 5, 0), roll(c, 3, 0)))

        def send(src, dst, row, side):
            pltpu.make_async_remote_copy(
                src, dst, halo_out.at[p], halo_in.at[there],
                device_id=place(side, row, target_group), device_id_type=MESH,
            ).start()

        send(pack.at[p, 2, :, 0], land.at[there, 4, :, 0], r_down, x_up)
        send(pack.at[p, 2, :, 1], land.at[there, 4, :, 1], r_up, x_up)
        send(pack.at[p, 2, :, 2], land.at[there, 4, :, 2], r_down, x_down)
        send(pack.at[p, 2, :, 3], land.at[there, 4, :, 3], r_up, x_down)
        send(field.at[f, :, 8:12, 0:8, :], land.at[there, 0], r, x_up)
        send(field.at[f, :, 4:8, 0:8, :], land.at[there, 1], r, x_down)
        send(pack.at[p, 0], land.at[there, 2], r_down, x)
        send(pack.at[p, 1], land.at[there, 3], r_up, x)

    def wait_on(ref, sem):
        pltpu.make_async_copy(ref, ref, sem).wait()

    def receive_halo(f):
        wait_on(land.at[f], halo_in.at[f])
        for k in range(2):
            for n in range(4):
                field[f, k, n, 0:8, :] = land[f, 0, k, n]
                field[f, k, 12 + n, 0:8, :] = land[f, 1, k, n]
            for t in range(4):
                a, b = land[f, 2, k, t], land[f, 3, k, t]
                field[f, k, 4 + 2 * t, 8:16, :] = jnp.where(half, a, roll(b, 4, 0))
                field[f, k, 5 + 2 * t, 8:16, :] = jnp.where(half, roll(a, 4, 0), b)
            for side, near in ((0, (3, 2, 1)), (1, (12, 13, 14))):
                a, b = land[f, 4, k, 2 * side], land[f, 4, k, 2 * side + 1]
                field[f, k, near[0], 8:16, :] = jnp.where(half, a, b)
                field[f, k, near[1], 8:16, :] = jnp.where(half, roll(a, 5, 0), roll(b, 3, 0))
                field[f, k, near[2], 8:16, :] = jnp.where(half, roll(a, 3, 0), roll(b, 5, 0))

    def sums(get, p, rows):
        result = []
        for k in range(2):
            m = get(k, p)
            c = m[:rows]
            s = get(k, p - 1)[:rows] + get(k, p + 1)[:rows]
            s = s + (roll(m, 1, 0)[:rows] + roll(m, -1, 0)[:rows])
            s = s + (roll(c, 1, 1) + roll(c, -1, 1))
            result.append((c, s))
        return result

    def update(middles, which, p, rows, h):
        (u, su), (v, sv) = middles
        reaction = (h * u) * (v * v) if h != 1.0 else u * (v * v)
        fa, fb, fc = (coef[which, n, p][:rows] for n in range(3))
        new_u = (fa * u + (h * diffusion_substrate) * su) + (fb - reaction)
        new_v = (fc * v + (h * diffusion_catalyst) * sv) + reaction
        return new_u, new_v

    def fine_step(get, store, lo, hi, whole):
        for p in range(lo, hi):
            rows = 16 if whole and lo < p < hi - 1 else 8
            new_u, new_v = update(sums(get, p, rows), 0, p, rows, time_step)
            store(0, p, rows, new_u)
            store(1, p, rows, new_v)

    def from_field(f):
        return lambda k, p: field[f, k, p]

    def from_work(w):
        return lambda k, p: work[w, k, p]

    def to_work(w):
        def store(k, p, rows, value):
            work[w, k, p, 0:rows, :] = value

        return store

    wait_on(block_of(COEF), block_in.at[COEF])
    send_halo(COEF, COEF, COEF, group)

    @pl.loop(0, SLOTS)
    def _(s):
        wait_on(block_of(s), block_in.at[s])
        send_halo(s, s, s, group)

    receive_halo(COEF)
    for which, h in ((0, time_step), (1, time_step * FACTOR)):
        for p in range(16):
            f, g = field[COEF, 0, p], field[COEF, 1, p]
            coef[which, 0, p] = (1.0 - 6.0 * h * diffusion_substrate) - h * f
            coef[which, 1, p] = h * f
            coef[which, 2, p] = (1.0 - 6.0 * h * diffusion_catalyst) - h * (f + g)

    @pl.loop(0, SLOTS)
    def _(s):
        receive_halo(s)
        fine_step(from_field(s), to_work(0), 1, 15, True)
        fine_step(from_work(0), to_work(1), 2, 14, True)
        fine_step(from_work(1), to_work(0), 3, 13, True)

        def store(k, p, rows, value):
            field[ENDS + s, k, p, 0:8, :] = value

        fine_step(from_work(0), store, 4, 12, False)
        send_halo(ENDS + s, ENDS + s, ENDS + s, group)

    my_rows = rows_of(r)

    def owner(turn_index, part):
        return turn_index, x * 4 + part

    def corrected_put(f, n, turn_index):
        for part in range(4):
            put(
                field.at[f, :, 4 + 2 * part : 6 + 2 * part, 0:8, :], corrected.at[0, :, :, my_rows, :],
                corr_out.at[n, part], corr_in, owner(turn_index, part),
            )

    def corrected_done(f, n, turn_index):
        for part in range(4):
            put_done(field.at[f, :, 4 + 2 * part : 6 + 2 * part, 0:8, :], corr_out.at[n, part], owner(turn_index, part))

    def residual_put(s):
        for part in range(4):
            put(
                diff.at[s, :, 2 * part : 2 * part + 2], residual.at[0, :, :, my_rows, :],
                diff_out.at[s, part], diff_in, owner(4 * group + s, part),
            )

    def residual_done(s):
        for part in range(4):
            put_done(diff.at[s, :, 2 * part : 2 * part + 2], diff_out.at[s, part], owner(4 * group + s, part))

    chain = core == 1
    chain_group = 2 * cube

    def defect_field(s):
        return jnp.where(cube == 0, START, DEFECT - 8) + 4 * group + s

    def has_halo(f):
        return jnp.logical_and(f != DEFECT + 3, f < DEFECT + 6)

    @pl.loop(0, SLOTS)
    def _(s):
        f = defect_field(s)
        receive_halo(ENDS + s)
        for p in range(1, 15):
            rows = 16 if 1 < p < 14 else 8
            middles = sums(from_field(ENDS + s), p, rows)
            new_u, new_v = update(middles, 0, p, rows, time_step)
            work[0, 0, p, 0:rows, :] = new_u
            work[0, 1, p, 0:rows, :] = new_v
            if 4 <= p < 12:
                new_u, new_v = update([(c[:8], w[:8]) for c, w in middles], 1, p, 8, time_step * FACTOR)
                coarse[0, p - 4] = new_u
                coarse[1, p - 4] = new_v
        fine_step(from_work(0), to_work(1), 2, 14, True)
        fine_step(from_work(1), to_work(0), 3, 13, True)
        opening = jnp.logical_and(group == 0, s == 0)
        following = jnp.minimum(s + 1, SLOTS - 1)

        def store(k, p, rows, value):
            late[s, k, p - 4] = value
            field[f, k, p, 0:8, :] = value - jnp.where(opening, 0.0, coarse[k, p - 4])
            diff[s + 1, k, p - 4] = value - field[ENDS + following, k, p, 0:8, :]

        fine_step(from_work(0), store, 4, 12, False)

        @pl.when(has_halo(f))
        def _():
            send_halo(f, f, f, chain_group)

        @pl.when(jnp.logical_and(core == 0, f < DEFECT + 7))
        def _():
            pltpu.make_async_remote_copy(
                block_of(f), block_of(f), block_out.at[f], block_in.at[f],
                device_id=place(x, r, chain_group), device_id_type=MESH,
            ).start()

        @pl.when(s < SLOTS - 1)
        def _():
            residual_put(s + 1)

        @pl.when(jnp.logical_and(s == SLOTS - 1, group < 3))
        def _():
            pltpu.make_async_remote_copy(
                late.at[s], back, back_out, back_in, device_id=place(x, r, group + 1), device_id_type=MESH
            ).start()

    def coarse_step(src, dst, d, lo, hi, whole):
        for p in range(lo, hi):
            rows = 16 if whole and lo < p < hi - 1 else 8
            new_u, new_v = update(sums(from_field(src), p, rows), 1, p, rows, time_step * FACTOR)
            field[dst, 0, p, 0:rows, :] = new_u + field[d, 0, p, 0:rows, :]
            field[dst, 1, p, 0:rows, :] = new_v + field[d, 1, p, 0:rows, :]

    steps = (START, TRAIL, TRAIL + 1, TRAIL + 2, MIDDLE, TRAIL + 3, TRAIL + 4, TRAIL + 5)
    first_turn = jnp.where(cube == 0, 1, 8)

    def first_residual():
        wait_on(back, back_in)
        for k in range(2):
            for b in range(8):
                diff[0, k, b] = back[k, b] - field[ENDS, k, 4 + b, 0:8, :]
        residual_put(0)

    @pl.when(chain)
    def _():
        @pl.when(cube == 0)
        def _():
            corrected_put(ENDS, 8, 0)

        @pl.when(cube == 1)
        def _():
            first_residual()

        for n in range(3):
            receive_halo(DEFECT + n)
        receive_halo(START)

        @pl.when(cube == 1)
        def _():
            wait_on(block_of(START), block_in.at[START])

        coarse_step(steps[0], steps[1], DEFECT, 1, 15, True)
        coarse_step(steps[1], steps[2], DEFECT + 1, 2, 14, True)
        coarse_step(steps[2], steps[3], DEFECT + 2, 3, 13, True)

        @pl.when(cube == 0)
        def _():
            wait_on(block_of(DEFECT + 3), block_in.at[DEFECT + 3])

        coarse_step(steps[3], steps[4], DEFECT + 3, 4, 12, False)
        send_halo(MIDDLE, MIDDLE, MIDDLE, group)

        @pl.when(cube == 0)
        def _():
            corrected_put(START, 0, 1)

        for n in range(1, 5):
            corrected_put(steps[n], n, first_turn + n)
        for n in range(4, 7):
            wait_on(block_of(DEFECT + n), block_in.at[DEFECT + n])
        for n in range(4, 6):
            receive_halo(DEFECT + n)
        receive_halo(MIDDLE)
        coarse_step(steps[4], steps[5], DEFECT + 4, 2, 14, True)
        coarse_step(steps[5], steps[6], DEFECT + 5, 3, 13, True)
        coarse_step(steps[6], steps[7], DEFECT + 6, 4, 12, False)

        @pl.when(cube == 0)
        def _():
            send_halo(steps[7], LAST_PACK, START, 2)
            pltpu.make_async_remote_copy(
                block_of(steps[7]), block_of(START), block_out.at[START], block_in.at[START],
                device_id=place(x, r, 2), device_id_type=MESH,
            ).start()

        for n in range(5, 8):
            corrected_put(steps[n], n, first_turn + n)

    @pl.when(core == 0)
    def _():
        first_residual()

    for other in range(4):
        for k, src in enumerate((feed, kill)):
            put_done(src.at[:, rows_of(coef_row), :], coef_out.at[other, k], place(x, coef_row, other))

    @pl.loop(0, 16)
    def _(i):
        row = lax.rem(r + i, 16)
        put_done(initial.at[:, :, rows_of(row), :], first_out.at[i], place(x, row, group_there))

    @pl.loop(0, ENDS + SLOTS)
    def _(f):
        wait_on(land.at[f], halo_out.at[f])

    @pl.loop(0, SLOTS)
    def _(s):
        f = defect_field(s)

        @pl.when(has_halo(f))
        def _():
            wait_on(land.at[f], halo_out.at[f])

        @pl.when(jnp.logical_and(core == 0, f < DEFECT + 7))
        def _():
            wait_on(block_of(f), block_out.at[f])

        @pl.when(4 * group + s > 0)
        def _():
            residual_done(s)

    @pl.when(group < 3)
    def _():
        wait_on(back, back_out)

    @pl.when(chain)
    def _():
        wait_on(land.at[MIDDLE], halo_out.at[MIDDLE])

        @pl.when(cube == 0)
        def _():
            wait_on(land.at[START], halo_out.at[LAST_PACK])
            wait_on(block_of(START), block_out.at[START])
            corrected_done(ENDS, 8, 0)
            corrected_done(START, 0, 1)

        for n in range(1, 8):
            corrected_done(steps[n], n, first_turn + n)

    wait_on(corrected, corr_in)

    @pl.when(tm > 0)
    def _():
        wait_on(residual, diff_in)

    @pl.when(tm == 0)
    def _():
        wait_on(residual.at[0], zero_sem)


def on_device(initial, estimate, feed_rate, kill_rate):
    dma = pltpu.SemaphoreType.DMA
    vmem = pltpu.VMEM
    return pl.pallas_call(
        kernel,
        out_shape=(jax.ShapeDtypeStruct(estimate.shape, F32), jax.ShapeDtypeStruct(estimate.shape, F32)),
        in_specs=[pl.BlockSpec(memory_space=pl.ANY)] * 4,
        out_specs=[pl.BlockSpec(memory_space=pl.ANY)] * 2,
        scratch_shapes=[
            vmem((FIELDS, 2, 16, 16, 128), F32),
            vmem((TRAIL, 5, 2, 4, 8, 128), F32),
            vmem((LAST_PACK + 1, 3, 2, 4, 8, 128), F32),
            vmem((2, 3, 16, 16, 128), F32),
            vmem((2, 2, 16, 16, 128), F32),
            vmem((SLOTS, 2, 8, 8, 128), F32),
            vmem((2, 8, 8, 128), F32),
            vmem((2, 8, 8, 128), F32),
            vmem((SLOTS + 1, 2, 8, 8, 128), F32),
            vmem((2, 2, 128, 128), F32),
            dma((TRAIL,)), dma((LAST_PACK + 1,)), dma((TRAIL,)), dma((TRAIL,)),
            dma((16,)), dma((4, 2)), dma((SLOTS, 4)), dma((9, 4)),
            dma, dma, dma, dma, dma,
        ],
        compiler_params=pltpu.CompilerParams(
            collective_id=0, has_side_effects=True, vmem_limit_bytes=40 * 1024 * 1024
        ),
        name="mgrit_cycle",
    )(initial, estimate, feed_rate, kill_rate)


def solution(mesh):
    placed = (
        P(None, "space", None, None),
        P("tm", None, "space", None, None),
        P("space", None, None),
        P("space", None, None),
    )
    return jax.shard_map(
        on_device,
        mesh=mesh,
        in_specs=placed,
        out_specs=(P("tm", None, "space", None, None), P("tm", None, "space", None, None)),
        check_vma=False,
    )
```

```python
import jax
import jax.numpy as jnp
from jax import lax
from jax.experimental import pallas as pl
from jax.experimental.pallas import tpu as pltpu
from jax.sharding import PartitionSpec as P

FACTOR = 4
time_step = 0.25
diffusion_substrate = 0.16
diffusion_catalyst = 0.08

MESH = pl.DeviceIdType.MESH
F32 = jnp.float32

STATE, COEF, ENDS, START, DEFECT, MIDDLE, TRAIL = 0, 4, 5, 9, 10, 17, 18
FIELDS = 24
SLOTS = 4
LAST_PACK = 18


def place(x, r, group):
    y = 2 * lax.div(group, 2) + lax.div(r, 8)
    z = jnp.where(r < 8, r, 15 - r)
    return y * 4 + lax.rem(z, 2) * 2 + 1 - lax.rem(group, 2), x * 4 + lax.div(z, 2)


def roll(value, by, axis):
    return pltpu.roll(value, by % value.shape[axis], axis)


def kernel(
    initial, estimate, feed, kill, corrected, residual,
    field, land, pack, coef, work, late, coarse, back, diff, zero,
    halo_in, halo_out, block_in, block_out, first_out, coef_out, diff_out, corr_out,
    diff_in, corr_in, back_in, back_out, zero_sem,
):
    tm = lax.axis_index("tm")
    space = lax.axis_index("space")
    x, z_hi = lax.div(space, 4), lax.rem(space, 4)
    y, z_lo, core = lax.div(tm, 4), lax.rem(lax.div(tm, 2), 2), lax.rem(tm, 2)
    z = 2 * z_hi + z_lo
    late_half = lax.div(y, 2)
    r = jnp.where(lax.rem(y, 2) == 0, z, 15 - z)
    group = 2 * late_half + 1 - core
    x_up, x_down = lax.rem(x + 1, 4), lax.rem(x + 3, 4)
    r_up, r_down = lax.rem(r + 1, 16), lax.rem(r + 15, 16)

    barrier = pltpu.get_barrier_semaphore()

    def greet(target):
        pl.semaphore_signal(barrier, inc=1, device_id=target, device_id_type=MESH)

    me = tm * 4 + z_hi

    @pl.loop(1, 64)
    def _(i):
        other = lax.rem(me + i, 64)
        greet((lax.div(other, 4), x * 4 + lax.rem(other, 4)))

    for side in (x_up, x_down):
        for row in (r_down, r, r_up):
            for other in range(4):
                greet(place(side, row, other))
    pl.semaphore_wait(barrier, 63 + 24)

    def is_me(target):
        return jnp.logical_and(target[0] == tm, target[1] == space)

    def put(src, dst, out_sem, in_sem, target):
        same = is_me(target)

        @pl.when(same)
        def _():
            pltpu.make_async_copy(src, dst, in_sem).start()

        @pl.when(jnp.logical_not(same))
        def _():
            pltpu.make_async_remote_copy(src, dst, out_sem, in_sem, device_id=target, device_id_type=MESH).start()

    def put_done(src, out_sem, target):
        @pl.when(jnp.logical_not(is_me(target)))
        def _():
            pltpu.make_async_copy(src, src, out_sem).wait()

    def rows_of(row):
        return pl.ds(pl.multiple_of(row * 8, 8), 8)

    here = pl.ds(4 + 2 * z_hi, 2)
    turn = lax.rem(tm + 1, 16)
    slot_there, group_there = lax.rem(turn, 4), lax.div(turn, 4)

    def coef_place(n):
        there = lax.rem(jnp.where(z_lo == 1, z + n, z + 8 - n), 8)
        row = jnp.where(lax.rem(y, 2) == 0, there, 15 - there)
        return row, (y * 4 + lax.rem(there, 2) * 2 + core, x * 4 + lax.div(there, 2))

    for n in range(4):
        row, target = coef_place(n)
        for k, src in enumerate((feed, kill)):
            put(src.at[:, rows_of(row), :], field.at[COEF, k, here, 0:8, :], coef_out.at[n, k], block_in.at[COEF], target)

    def first_put(src):
        @pl.loop(0, 16)
        def _(i):
            row = lax.rem(r + i, 16)
            put(
                src.at[:, :, rows_of(row), :], field.at[slot_there, :, here, 0:8, :],
                first_out.at[i], block_in.at[slot_there], place(x, row, group_there),
            )

    @pl.when(tm < 15)
    def _():
        first_put(estimate.at[0])

    @pl.when(tm == 15)
    def _():
        first_put(initial)

    @pl.when(tm == 0)
    def _():
        zero[...] = jnp.zeros_like(zero)
        pltpu.make_async_copy(zero, residual.at[0], zero_sem).start()

    low = lax.broadcasted_iota(jnp.int32, (8, 128), 0)
    half = low < 4

    def block_of(f):
        return field.at[f, :, 4:12, 0:8, :]

    def send_halo(f, p, there, target_group):
        for k in range(2):
            plane = [field[f, k, 4 + b, 0:8, :] for b in range(8)]
            for t in range(4):
                a, b = plane[2 * t], plane[2 * t + 1]
                pack[p, 0, k, t] = jnp.where(half, a, roll(b, 4, 0))
                pack[p, 1, k, t] = jnp.where(half, roll(a, 4, 0), b)
            for side, near in ((0, (7, 6, 5)), (1, (0, 1, 2))):
                a, b, c = (plane[n] for n in near)
                pack[p, 2, k, 2 * side] = jnp.where(low < 3, a, jnp.where(low < 5, roll(b, 3, 0), roll(c, 5, 0)))
                pack[p, 2, k, 2 * side + 1] = jnp.where(low >= 5, a, jnp.where(low >= 3, roll(b, 5, 0), roll(c, 3, 0)))

        def send(src, dst, row, side):
            pltpu.make_async_remote_copy(
                src, dst, halo_out.at[p], halo_in.at[there],
                device_id=place(side, row, target_group), device_id_type=MESH,
            ).start()

        send(pack.at[p, 2, :, 0], land.at[there, 4, :, 0], r_down, x_up)
        send(pack.at[p, 2, :, 1], land.at[there, 4, :, 1], r_up, x_up)
        send(pack.at[p, 2, :, 2], land.at[there, 4, :, 2], r_down, x_down)
        send(pack.at[p, 2, :, 3], land.at[there, 4, :, 3], r_up, x_down)
        send(field.at[f, :, 8:12, 0:8, :], land.at[there, 0], r, x_up)
        send(field.at[f, :, 4:8, 0:8, :], land.at[there, 1], r, x_down)
        send(pack.at[p, 0], land.at[there, 2], r_down, x)
        send(pack.at[p, 1], land.at[there, 3], r_up, x)

    def wait_on(ref, sem):
        pltpu.make_async_copy(ref, ref, sem).wait()

    def receive_halo(f):
        wait_on(land.at[f], halo_in.at[f])
        for k in range(2):
            for n in range(4):
                field[f, k, n, 0:8, :] = land[f, 0, k, n]
                field[f, k, 12 + n, 0:8, :] = land[f, 1, k, n]
            for t in range(4):
                a, b = land[f, 2, k, t], land[f, 3, k, t]
                field[f, k, 4 + 2 * t, 8:16, :] = jnp.where(half, a, roll(b, 4, 0))
                field[f, k, 5 + 2 * t, 8:16, :] = jnp.where(half, roll(a, 4, 0), b)
            for side, near in ((0, (3, 2, 1)), (1, (12, 13, 14))):
                a, b = land[f, 4, k, 2 * side], land[f, 4, k, 2 * side + 1]
                field[f, k, near[0], 8:16, :] = jnp.where(half, a, b)
                field[f, k, near[1], 8:16, :] = jnp.where(half, roll(a, 5, 0), roll(b, 3, 0))
                field[f, k, near[2], 8:16, :] = jnp.where(half, roll(a, 3, 0), roll(b, 5, 0))

    def sums(get, p, rows):
        result = []
        for k in range(2):
            m = get(k, p)
            c = m[:rows]
            s = get(k, p - 1)[:rows] + get(k, p + 1)[:rows]
            s = s + (roll(m, 1, 0)[:rows] + roll(m, -1, 0)[:rows])
            s = s + (roll(c, 1, 1) + roll(c, -1, 1))
            result.append((c, s))
        return result

    def update(middles, which, p, rows, h):
        (u, su), (v, sv) = middles
        reaction = (h * u) * (v * v) if h != 1.0 else u * (v * v)
        fa, fb, fc = (coef[which, n, p][:rows] for n in range(3))
        new_u = (fa * u + (h * diffusion_substrate) * su) + (fb - reaction)
        new_v = (fc * v + (h * diffusion_catalyst) * sv) + reaction
        return new_u, new_v

    def fine_step(get, store, lo, hi, whole):
        for p in range(lo, hi):
            rows = 16 if whole and lo < p < hi - 1 else 8
            new_u, new_v = update(sums(get, p, rows), 0, p, rows, time_step)
            store(0, p, rows, new_u)
            store(1, p, rows, new_v)

    def from_field(f):
        return lambda k, p: field[f, k, p]

    def from_work(w):
        return lambda k, p: work[w, k, p]

    def to_work(w):
        def store(k, p, rows, value):
            work[w, k, p, 0:rows, :] = value

        return store

    wait_on(block_of(COEF), block_in.at[COEF])
    send_halo(COEF, COEF, COEF, group)

    @pl.loop(0, SLOTS)
    def _(s):
        wait_on(block_of(s), block_in.at[s])
        send_halo(s, s, s, group)

    receive_halo(COEF)
    for which, h in ((0, time_step), (1, time_step * FACTOR)):
        for p in range(16):
            f, g = field[COEF, 0, p], field[COEF, 1, p]
            coef[which, 0, p] = (1.0 - 6.0 * h * diffusion_substrate) - h * f
            coef[which, 1, p] = h * f
            coef[which, 2, p] = (1.0 - 6.0 * h * diffusion_catalyst) - h * (f + g)

    @pl.loop(0, SLOTS)
    def _(s):
        receive_halo(s)
        fine_step(from_field(s), to_work(0), 1, 15, True)
        fine_step(from_work(0), to_work(1), 2, 14, True)
        fine_step(from_work(1), to_work(0), 3, 13, True)

        def store(k, p, rows, value):
            field[ENDS + s, k, p, 0:8, :] = value

        fine_step(from_work(0), store, 4, 12, False)
        send_halo(ENDS + s, ENDS + s, ENDS + s, group)

    my_rows = rows_of(r)

    def owner(turn_index, part):
        return turn_index, x * 4 + part

    def corrected_put(f, n, turn_index):
        for part in range(4):
            put(
                field.at[f, :, 4 + 2 * part : 6 + 2 * part, 0:8, :], corrected.at[0, :, :, my_rows, :],
                corr_out.at[n, part], corr_in, owner(turn_index, part),
            )

    def corrected_done(f, n, turn_index):
        for part in range(4):
            put_done(field.at[f, :, 4 + 2 * part : 6 + 2 * part, 0:8, :], corr_out.at[n, part], owner(turn_index, part))

    def residual_put(s):
        for part in range(4):
            put(
                diff.at[s, :, 2 * part : 2 * part + 2], residual.at[0, :, :, my_rows, :],
                diff_out.at[s, part], diff_in, owner(4 * group + s, part),
            )

    def residual_done(s):
        for part in range(4):
            put_done(diff.at[s, :, 2 * part : 2 * part + 2], diff_out.at[s, part], owner(4 * group + s, part))

    chain = core == 1
    chain_group = 2 * late_half

    def defect_field(s):
        return jnp.where(late_half == 0, START, DEFECT - 8) + 4 * group + s

    def has_halo(f):
        return jnp.logical_and(f != DEFECT + 3, f < DEFECT + 6)

    @pl.loop(0, SLOTS)
    def _(s):
        f = defect_field(s)
        receive_halo(ENDS + s)
        for p in range(1, 15):
            rows = 16 if 1 < p < 14 else 8
            middles = sums(from_field(ENDS + s), p, rows)
            new_u, new_v = update(middles, 0, p, rows, time_step)
            work[0, 0, p, 0:rows, :] = new_u
            work[0, 1, p, 0:rows, :] = new_v
            if 4 <= p < 12:
                new_u, new_v = update([(c[:8], w[:8]) for c, w in middles], 1, p, 8, time_step * FACTOR)
                coarse[0, p - 4] = new_u
                coarse[1, p - 4] = new_v
        fine_step(from_work(0), to_work(1), 2, 14, True)
        fine_step(from_work(1), to_work(0), 3, 13, True)
        opening = jnp.logical_and(group == 0, s == 0)
        following = jnp.minimum(s + 1, SLOTS - 1)

        def store(k, p, rows, value):
            late[s, k, p - 4] = value
            field[f, k, p, 0:8, :] = value - jnp.where(opening, 0.0, coarse[k, p - 4])
            diff[s + 1, k, p - 4] = value - field[ENDS + following, k, p, 0:8, :]

        fine_step(from_work(0), store, 4, 12, False)

        @pl.when(has_halo(f))
        def _():
            send_halo(f, f, f, chain_group)

        @pl.when(jnp.logical_and(core == 0, f < DEFECT + 7))
        def _():
            pltpu.make_async_remote_copy(
                block_of(f), block_of(f), block_out.at[f], block_in.at[f],
                device_id=place(x, r, chain_group), device_id_type=MESH,
            ).start()

        @pl.when(s < SLOTS - 1)
        def _():
            residual_put(s + 1)

        @pl.when(jnp.logical_and(s == SLOTS - 1, group < 3))
        def _():
            pltpu.make_async_remote_copy(
                late.at[s], back, back_out, back_in, device_id=place(x, r, group + 1), device_id_type=MESH
            ).start()

    def coarse_step(src, dst, d, lo, hi, whole):
        for p in range(lo, hi):
            rows = 16 if whole and lo < p < hi - 1 else 8
            new_u, new_v = update(sums(from_field(src), p, rows), 1, p, rows, time_step * FACTOR)
            field[dst, 0, p, 0:rows, :] = new_u + field[d, 0, p, 0:rows, :]
            field[dst, 1, p, 0:rows, :] = new_v + field[d, 1, p, 0:rows, :]

    steps = (START, TRAIL, TRAIL + 1, TRAIL + 2, MIDDLE, TRAIL + 3, TRAIL + 4, TRAIL + 5)
    first_turn = jnp.where(late_half == 0, 1, 8)

    def first_residual():
        wait_on(back, back_in)
        for k in range(2):
            for b in range(8):
                diff[0, k, b] = back[k, b] - field[ENDS, k, 4 + b, 0:8, :]
        residual_put(0)

    @pl.when(chain)
    def _():
        @pl.when(late_half == 0)
        def _():
            corrected_put(ENDS, 8, 0)

        @pl.when(late_half == 1)
        def _():
            first_residual()

        for n in range(3):
            receive_halo(DEFECT + n)
        receive_halo(START)

        @pl.when(late_half == 1)
        def _():
            wait_on(block_of(START), block_in.at[START])

        coarse_step(steps[0], steps[1], DEFECT, 1, 15, True)
        coarse_step(steps[1], steps[2], DEFECT + 1, 2, 14, True)
        coarse_step(steps[2], steps[3], DEFECT + 2, 3, 13, True)

        @pl.when(late_half == 0)
        def _():
            wait_on(block_of(DEFECT + 3), block_in.at[DEFECT + 3])

        coarse_step(steps[3], steps[4], DEFECT + 3, 4, 12, False)
        send_halo(MIDDLE, MIDDLE, MIDDLE, group)

        @pl.when(late_half == 0)
        def _():
            corrected_put(START, 0, 1)

        for n in range(1, 5):
            corrected_put(steps[n], n, first_turn + n)
        for n in range(4, 7):
            wait_on(block_of(DEFECT + n), block_in.at[DEFECT + n])
        for n in range(4, 6):
            receive_halo(DEFECT + n)
        receive_halo(MIDDLE)
        coarse_step(steps[4], steps[5], DEFECT + 4, 2, 14, True)
        coarse_step(steps[5], steps[6], DEFECT + 5, 3, 13, True)
        coarse_step(steps[6], steps[7], DEFECT + 6, 4, 12, False)

        @pl.when(late_half == 0)
        def _():
            send_halo(steps[7], LAST_PACK, START, 2)
            pltpu.make_async_remote_copy(
                block_of(steps[7]), block_of(START), block_out.at[START], block_in.at[START],
                device_id=place(x, r, 2), device_id_type=MESH,
            ).start()

        for n in range(5, 8):
            corrected_put(steps[n], n, first_turn + n)

    @pl.when(core == 0)
    def _():
        first_residual()

    for n in range(4):
        row, target = coef_place(n)
        for k, src in enumerate((feed, kill)):
            put_done(src.at[:, rows_of(row), :], coef_out.at[n, k], target)

    @pl.loop(0, 16)
    def _(i):
        row = lax.rem(r + i, 16)
        put_done(initial.at[:, :, rows_of(row), :], first_out.at[i], place(x, row, group_there))

    @pl.loop(0, ENDS + SLOTS)
    def _(f):
        wait_on(land.at[f], halo_out.at[f])

    @pl.loop(0, SLOTS)
    def _(s):
        f = defect_field(s)

        @pl.when(has_halo(f))
        def _():
            wait_on(land.at[f], halo_out.at[f])

        @pl.when(jnp.logical_and(core == 0, f < DEFECT + 7))
        def _():
            wait_on(block_of(f), block_out.at[f])

        @pl.when(4 * group + s > 0)
        def _():
            residual_done(s)

    @pl.when(group < 3)
    def _():
        wait_on(back, back_out)

    @pl.when(chain)
    def _():
        wait_on(land.at[MIDDLE], halo_out.at[MIDDLE])

        @pl.when(late_half == 0)
        def _():
            wait_on(land.at[START], halo_out.at[LAST_PACK])
            wait_on(block_of(START), block_out.at[START])
            corrected_done(ENDS, 8, 0)
            corrected_done(START, 0, 1)

        for n in range(1, 8):
            corrected_done(steps[n], n, first_turn + n)

    wait_on(corrected, corr_in)

    @pl.when(tm > 0)
    def _():
        wait_on(residual, diff_in)

    @pl.when(tm == 0)
    def _():
        wait_on(residual.at[0], zero_sem)


def on_device(initial, estimate, feed_rate, kill_rate):
    dma = pltpu.SemaphoreType.DMA
    vmem = pltpu.VMEM
    return pl.pallas_call(
        kernel,
        out_shape=(jax.ShapeDtypeStruct(estimate.shape, F32), jax.ShapeDtypeStruct(estimate.shape, F32)),
        in_specs=[pl.BlockSpec(memory_space=pl.ANY)] * 4,
        out_specs=[pl.BlockSpec(memory_space=pl.ANY)] * 2,
        scratch_shapes=[
            vmem((FIELDS, 2, 16, 16, 128), F32),
            vmem((TRAIL, 5, 2, 4, 8, 128), F32),
            vmem((LAST_PACK + 1, 3, 2, 4, 8, 128), F32),
            vmem((2, 3, 16, 16, 128), F32),
            vmem((2, 2, 16, 16, 128), F32),
            vmem((SLOTS, 2, 8, 8, 128), F32),
            vmem((2, 8, 8, 128), F32),
            vmem((2, 8, 8, 128), F32),
            vmem((SLOTS + 1, 2, 8, 8, 128), F32),
            vmem((2, 2, 128, 128), F32),
            dma((TRAIL,)), dma((LAST_PACK + 1,)), dma((TRAIL,)), dma((TRAIL,)),
            dma((16,)), dma((4, 2)), dma((SLOTS, 4)), dma((9, 4)),
            dma, dma, dma, dma, dma,
        ],
        compiler_params=pltpu.CompilerParams(
            collective_id=0, has_side_effects=True, vmem_limit_bytes=63 * 1024 * 1024
        ),
        name="mgrit_cycle",
    )(initial, estimate, feed_rate, kill_rate)


def solution(mesh):
    placed = (
        P(None, "space", None, None),
        P("tm", None, "space", None, None),
        P("space", None, None),
        P("space", None, None),
    )
    return jax.shard_map(
        on_device,
        mesh=mesh,
        in_specs=placed,
        out_specs=(P("tm", None, "space", None, None), P("tm", None, "space", None, None)),
        check_vma=False,
    )
```

```python
import jax
import jax.numpy as jnp
from jax import lax
from jax.experimental import pallas as pl
from jax.experimental.pallas import tpu as pltpu
from jax.sharding import PartitionSpec as P

FACTOR = 4
time_step = 0.25
diffusion_substrate = 0.16
diffusion_catalyst = 0.08

MESH = pl.DeviceIdType.MESH
F32 = jnp.float32

STATE, COEF, ENDS, START, DEFECT, MIDDLE, TRAIL = 0, 4, 5, 9, 10, 17, 18
FIELDS = 24
SLOTS = 4
LAST_PACK = 18


def place(x, r, group):
    y = 2 * lax.div(group, 2) + lax.div(r, 8)
    z = jnp.where(r < 8, r, 15 - r)
    return y * 4 + lax.rem(z, 2) * 2 + 1 - lax.rem(group, 2), x * 4 + lax.div(z, 2)


def roll(value, by, axis):
    return pltpu.roll(value, by % value.shape[axis], axis)


def kernel(
    initial, estimate, feed, kill, both,
    field, land, pack, coef, work, late, coarse, back, diff, zero,
    halo_in, halo_out, block_in, block_out, first_out, coef_out, diff_out, corr_out,
    diff_in, corr_in, back_in, back_out, zero_sem, go,
):
    corrected, residual = both.at[0], both.at[1]
    tm = lax.axis_index("tm")
    space = lax.axis_index("space")
    x, z_hi = lax.div(space, 4), lax.rem(space, 4)
    y, z_lo, core = lax.div(tm, 4), lax.rem(lax.div(tm, 2), 2), lax.rem(tm, 2)
    z = 2 * z_hi + z_lo
    late_half = lax.div(y, 2)
    r = jnp.where(lax.rem(y, 2) == 0, z, 15 - z)
    group = 2 * late_half + 1 - core
    x_up, x_down = lax.rem(x + 1, 4), lax.rem(x + 3, 4)
    r_up, r_down = lax.rem(r + 1, 16), lax.rem(r + 15, 16)

    near = {}
    for dx, side in ((-1, x_down), (0, x), (1, x_up)):
        for dr, row in ((-1, r_down), (0, r), (1, r_up)):
            near[dx, dr] = place(side, row, 2 * late_half + 1)

    def neighbour(dx, dr, offset):
        base, part = near[dx, dr]
        return base + offset, part

    barrier = pltpu.get_barrier_semaphore()

    def is_me(target):
        return jnp.logical_and(target[0] == tm, target[1] == space)

    turn = lax.rem(tm + 1, 16)
    slot_there, group_there = lax.rem(turn, 4), lax.div(turn, 4)

    def greet(target):
        pl.semaphore_signal(barrier, inc=1, device_id=target, device_id_type=MESH)

    def greet_other(target):
        @pl.when(jnp.logical_not(is_me(target)))
        def _():
            greet(target)

    @pl.loop(0, 16)
    def _(i):
        greet_other((lax.rem(4 * group + lax.div(i, 4) + 15, 16), x * 4 + lax.rem(i, 4)))

    ahead = 2 * z_lo - 1
    for n in (1, -2, 3):
        there = lax.rem(z + n * ahead + 8, 8)
        greet((y * 4 + lax.rem(there, 2) * 2 + core, x * 4 + lax.div(there, 2)))

    for dx in (-1, 0, 1):
        for dr in (-1, 0, 1):
            if dx or dr:
                greet(neighbour(dx, dr, core))
    greet((tm + 1 - 2 * core, space))

    @pl.when(jnp.logical_and(late_half == 1, core == 1))
    def _():
        greet((tm - 8, space))
        greet((tm - 9, space))

    @pl.when(lax.rem(tm, 4) == 3)
    def _():
        @pl.loop(0, 16)
        def _(i):
            greet_other(place(x, i, lax.div(tm, 4)))

    mine_there = (group_there == group).astype(jnp.int32)
    mine_last = jnp.logical_and(lax.rem(tm, 4) == 3, lax.div(tm, 4) == group).astype(jnp.int32)
    pl.semaphore_wait(barrier, (16 - mine_there) + 3 + 8 + 1 + (1 - late_half) + (4 - mine_last))

    def put(src, dst, out_sem, in_sem, target):
        same = is_me(target)

        @pl.when(same)
        def _():
            pltpu.make_async_copy(src, dst, in_sem).start()

        @pl.when(jnp.logical_not(same))
        def _():
            pltpu.make_async_remote_copy(src, dst, out_sem, in_sem, device_id=target, device_id_type=MESH).start()

    def put_done(src, out_sem, target):
        @pl.when(jnp.logical_not(is_me(target)))
        def _():
            pltpu.make_async_copy(src, src, out_sem).wait()

    def rows_of(row):
        return pl.ds(pl.multiple_of(row * 8, 8), 8)

    here = pl.ds(4 + 2 * z_hi, 2)

    def coef_place(n):
        there = lax.rem(jnp.where(z_lo == 1, z + n, z + 8 - n), 8)
        row = jnp.where(lax.rem(y, 2) == 0, there, 15 - there)
        return row, (y * 4 + lax.rem(there, 2) * 2 + core, x * 4 + lax.div(there, 2))

    for n in range(4):
        row, target = coef_place(n)
        for k, src in enumerate((feed, kill)):
            put(src.at[:, rows_of(row), :], field.at[COEF, k, here, 0:8, :], coef_out.at[n, k], block_in.at[COEF], target)

    def first_row(i):
        n = lax.div(i, 2)
        step = jnp.where(lax.rem(n, 2) == 1, 4 - lax.div(n + 1, 2), 4 + lax.div(n, 2))
        there = lax.rem(z + step, 8)
        return jnp.where(lax.rem(i, 2) == 0, there, 15 - there)

    def first_put(src):
        @pl.loop(0, 16)
        def _(i):
            row = first_row(i)
            put(
                src.at[:, :, rows_of(row), :], field.at[slot_there, :, here, 0:8, :],
                first_out.at[i], block_in.at[slot_there], place(x, row, group_there),
            )

    @pl.when(tm < 15)
    def _():
        first_put(estimate.at[0])

    @pl.when(tm == 15)
    def _():
        first_put(initial)

    @pl.when(tm == 0)
    def _():
        zero[...] = jnp.zeros_like(zero)
        pltpu.make_async_copy(zero, residual.at[0], zero_sem).start()

    low = lax.broadcasted_iota(jnp.int32, (8, 128), 0)
    half = low < 4

    def block_of(f):
        return field.at[f, :, 4:12, 0:8, :]

    def send_halo(f, p, there, offset):
        for k in range(2):
            plane = [field[f, k, 4 + b, 0:8, :] for b in range(8)]
            for t in range(4):
                a, b = plane[2 * t], plane[2 * t + 1]
                pack[p, 0, k, t] = jnp.where(half, a, roll(b, 4, 0))
                pack[p, 1, k, t] = jnp.where(half, roll(a, 4, 0), b)
            for side, near in ((0, (7, 6, 5)), (1, (0, 1, 2))):
                a, b, c = (plane[n] for n in near)
                pack[p, 2, k, 2 * side] = jnp.where(low < 3, a, jnp.where(low < 5, roll(b, 3, 0), roll(c, 5, 0)))
                pack[p, 2, k, 2 * side + 1] = jnp.where(low >= 5, a, jnp.where(low >= 3, roll(b, 5, 0), roll(c, 3, 0)))

        def send(src, dst, dx, dr):
            pltpu.make_async_remote_copy(
                src, dst, halo_out.at[p], halo_in.at[there],
                device_id=neighbour(dx, dr, offset), device_id_type=MESH,
            ).start()

        send(pack.at[p, 2, :, 0], land.at[there, 4, :, 0], 1, -1)
        send(pack.at[p, 2, :, 1], land.at[there, 4, :, 1], 1, 1)
        send(pack.at[p, 2, :, 2], land.at[there, 4, :, 2], -1, -1)
        send(pack.at[p, 2, :, 3], land.at[there, 4, :, 3], -1, 1)
        send(field.at[f, :, 8:12, 0:8, :], land.at[there, 0], 1, 0)
        send(field.at[f, :, 4:8, 0:8, :], land.at[there, 1], -1, 0)
        send(pack.at[p, 0], land.at[there, 2], 0, -1)
        send(pack.at[p, 1], land.at[there, 3], 0, 1)

    def wait_on(ref, sem):
        pltpu.make_async_copy(ref, ref, sem).wait()

    def receive_halo(f):
        wait_on(land.at[f], halo_in.at[f])
        for k in range(2):
            for n in range(4):
                field[f, k, n, 0:8, :] = land[f, 0, k, n]
                field[f, k, 12 + n, 0:8, :] = land[f, 1, k, n]
            for t in range(4):
                a, b = land[f, 2, k, t], land[f, 3, k, t]
                field[f, k, 4 + 2 * t, 8:16, :] = jnp.where(half, a, roll(b, 4, 0))
                field[f, k, 5 + 2 * t, 8:16, :] = jnp.where(half, roll(a, 4, 0), b)
            for side, near in ((0, (3, 2, 1)), (1, (12, 13, 14))):
                a, b = land[f, 4, k, 2 * side], land[f, 4, k, 2 * side + 1]
                field[f, k, near[0], 8:16, :] = jnp.where(half, a, b)
                field[f, k, near[1], 8:16, :] = jnp.where(half, roll(a, 5, 0), roll(b, 3, 0))
                field[f, k, near[2], 8:16, :] = jnp.where(half, roll(a, 3, 0), roll(b, 5, 0))

    def sums(get, p, rows):
        result = []
        for k in range(2):
            m = get(k, p)
            c = m[:rows]
            s = get(k, p - 1)[:rows] + get(k, p + 1)[:rows]
            s = s + (roll(m, 1, 0)[:rows] + roll(m, -1, 0)[:rows])
            s = s + (roll(c, 1, 1) + roll(c, -1, 1))
            result.append((c, s))
        return result

    def update(middles, which, p, rows, h):
        (u, su), (v, sv) = middles
        reaction = (h * u) * (v * v) if h != 1.0 else u * (v * v)
        fa, fb, fc = (coef[which, n, p][:rows] for n in range(3))
        new_u = (fa * u + (h * diffusion_substrate) * su) + (fb - reaction)
        new_v = (fc * v + (h * diffusion_catalyst) * sv) + reaction
        return new_u, new_v

    def fine_step(get, store, lo, hi, whole):
        for p in range(lo, hi):
            rows = 16 if whole and lo < p < hi - 1 else 8
            new_u, new_v = update(sums(get, p, rows), 0, p, rows, time_step)
            store(0, p, rows, new_u)
            store(1, p, rows, new_v)

    def from_field(f):
        return lambda k, p: field[f, k, p]

    def from_work(w):
        return lambda k, p: work[w, k, p]

    def to_work(w):
        def store(k, p, rows, value):
            work[w, k, p, 0:rows, :] = value

        return store

    wait_on(block_of(COEF), block_in.at[COEF])
    send_halo(COEF, COEF, COEF, core)

    @pl.loop(0, SLOTS)
    def _(s):
        wait_on(block_of(s), block_in.at[s])
        send_halo(s, s, s, core)

    receive_halo(COEF)
    for which, h in ((0, time_step), (1, time_step * FACTOR)):
        for p in range(16):
            f, g = field[COEF, 0, p], field[COEF, 1, p]
            coef[which, 0, p] = (1.0 - 6.0 * h * diffusion_substrate) - h * f
            coef[which, 1, p] = h * f
            coef[which, 2, p] = (1.0 - 6.0 * h * diffusion_catalyst) - h * (f + g)

    @pl.loop(0, SLOTS)
    def _(s):
        receive_halo(s)
        fine_step(from_field(s), to_work(0), 1, 15, True)
        fine_step(from_work(0), to_work(1), 2, 14, True)
        fine_step(from_work(1), to_work(0), 3, 13, True)

        def store(k, p, rows, value):
            field[ENDS + s, k, p, 0:8, :] = value

        fine_step(from_work(0), store, 4, 12, False)
        send_halo(ENDS + s, ENDS + s, ENDS + s, core)

    my_rows = rows_of(r)

    def owner(turn_index, part):
        return turn_index, x * 4 + part

    def corrected_put(f, n, turn_index):
        for part in range(4):
            put(
                field.at[f, :, 4 + 2 * part : 6 + 2 * part, 0:8, :], corrected.at[0, :, :, my_rows, :],
                corr_out.at[n, part], corr_in, owner(turn_index, part),
            )

    def corrected_done(f, n, turn_index):
        for part in range(4):
            put_done(field.at[f, :, 4 + 2 * part : 6 + 2 * part, 0:8, :], corr_out.at[n, part], owner(turn_index, part))

    def residual_put(s):
        for part in range(4):
            put(
                diff.at[s, :, 2 * part : 2 * part + 2], residual.at[0, :, :, my_rows, :],
                diff_out.at[s, part], diff_in, owner(4 * group + s, part),
            )

    def residual_done(s):
        for part in range(4):
            put_done(diff.at[s, :, 2 * part : 2 * part + 2], diff_out.at[s, part], owner(4 * group + s, part))

    chain = core == 1
    chain_group = 2 * late_half

    def defect_field(s):
        return jnp.where(late_half == 0, START, DEFECT - 8) + 4 * group + s

    def has_halo(f):
        return jnp.logical_and(f != DEFECT + 3, f < DEFECT + 6)

    @pl.when(group == 0)
    def _():
        corrected_put(ENDS, 8, 0)

    @pl.loop(0, SLOTS)
    def _(s):
        f = defect_field(s)
        receive_halo(ENDS + s)
        for p in range(1, 15):
            rows = 16 if 1 < p < 14 else 8
            middles = sums(from_field(ENDS + s), p, rows)
            new_u, new_v = update(middles, 0, p, rows, time_step)
            work[0, 0, p, 0:rows, :] = new_u
            work[0, 1, p, 0:rows, :] = new_v
            if 4 <= p < 12:
                new_u, new_v = update([(c[:8], w[:8]) for c, w in middles], 1, p, 8, time_step * FACTOR)
                coarse[0, p - 4] = new_u
                coarse[1, p - 4] = new_v
        fine_step(from_work(0), to_work(1), 2, 14, True)
        fine_step(from_work(1), to_work(0), 3, 13, True)
        opening = jnp.logical_and(group == 0, s == 0)
        following = jnp.minimum(s + 1, SLOTS - 1)

        def store(k, p, rows, value):
            late[s, k, p - 4] = value
            field[f, k, p, 0:8, :] = value - jnp.where(opening, 0.0, coarse[k, p - 4])
            diff[s + 1, k, p - 4] = value - field[ENDS + following, k, p, 0:8, :]

        fine_step(from_work(0), store, 4, 12, False)

        @pl.when(has_halo(f))
        def _():
            send_halo(f, f, f, 1)

        @pl.when(jnp.logical_and(core == 0, f < DEFECT + 7))
        def _():
            pltpu.make_async_remote_copy(
                block_of(f), block_of(f), block_out.at[f], block_in.at[f],
                device_id=place(x, r, chain_group), device_id_type=MESH,
            ).start()

        @pl.when(jnp.logical_and(s < SLOTS - 1, late_half == 1))
        def _():
            residual_put(s + 1)

        @pl.when(jnp.logical_and(s == SLOTS - 1, group < 3))
        def _():
            pltpu.make_async_remote_copy(
                late.at[s], back, back_out, back_in, device_id=place(x, r, group + 1), device_id_type=MESH
            ).start()

    def coarse_step(src, dst, d, lo, hi, whole):
        for p in range(lo, hi):
            rows = 16 if whole and lo < p < hi - 1 else 8
            new_u, new_v = update(sums(from_field(src), p, rows), 1, p, rows, time_step * FACTOR)
            field[dst, 0, p, 0:rows, :] = new_u + field[d, 0, p, 0:rows, :]
            field[dst, 1, p, 0:rows, :] = new_v + field[d, 1, p, 0:rows, :]

    steps = (START, TRAIL, TRAIL + 1, TRAIL + 2, MIDDLE, TRAIL + 3, TRAIL + 4, TRAIL + 5)
    first_turn = jnp.where(late_half == 0, 1, 8)

    def first_residual():
        wait_on(back, back_in)
        for k in range(2):
            for b in range(8):
                diff[0, k, b] = back[k, b] - field[ENDS, k, 4 + b, 0:8, :]
        residual_put(0)

    @pl.when(chain)
    def _():
        @pl.when(late_half == 1)
        def _():
            first_residual()

        for n in range(3):
            receive_halo(DEFECT + n)
        receive_halo(START)

        @pl.when(late_half == 1)
        def _():
            wait_on(block_of(START), block_in.at[START])

        coarse_step(steps[0], steps[1], DEFECT, 1, 15, True)
        coarse_step(steps[1], steps[2], DEFECT + 1, 2, 14, True)
        coarse_step(steps[2], steps[3], DEFECT + 2, 3, 13, True)

        @pl.when(late_half == 0)
        def _():
            wait_on(block_of(DEFECT + 3), block_in.at[DEFECT + 3])

        coarse_step(steps[3], steps[4], DEFECT + 3, 4, 12, False)
        send_halo(MIDDLE, MIDDLE, MIDDLE, core)

        for n in range(4, 7):
            wait_on(block_of(DEFECT + n), block_in.at[DEFECT + n])

        @pl.when(late_half == 1)
        def _():
            for n in range(0, 5):
                corrected_put(steps[n], n, first_turn + n)

        for n in range(4, 6):
            receive_halo(DEFECT + n)
        receive_halo(MIDDLE)
        coarse_step(steps[4], steps[5], DEFECT + 4, 2, 14, True)

        @pl.when(late_half == 1)
        def _():
            corrected_put(steps[5], 5, first_turn + 5)

        coarse_step(steps[5], steps[6], DEFECT + 5, 3, 13, True)

        @pl.when(late_half == 1)
        def _():
            corrected_put(steps[6], 6, first_turn + 6)

        coarse_step(steps[6], steps[7], DEFECT + 6, 4, 12, False)

        @pl.when(late_half == 0)
        def _():
            send_halo(steps[7], LAST_PACK, START, 9)
            pltpu.make_async_remote_copy(
                block_of(steps[7]), block_of(START), block_out.at[START], block_in.at[START],
                device_id=place(x, r, 2), device_id_type=MESH,
            ).start()
            pl.semaphore_signal(go, inc=1, device_id=(tm - 1, space), device_id_type=MESH)
            for n in range(0, 7):
                corrected_put(steps[n], n, first_turn + n)

        @pl.when(late_half == 1)
        def _():
            corrected_put(steps[7], 7, first_turn + 7)

        @pl.when(late_half == 0)
        def _():
            for n in range(1, SLOTS):
                residual_put(n)

    @pl.when(jnp.logical_and(core == 0, late_half == 0))
    def _():
        pl.semaphore_wait(go, 1)
        for n in range(1, SLOTS):
            residual_put(n)

    @pl.when(core == 0)
    def _():
        first_residual()

    for n in range(4):
        row, target = coef_place(n)
        for k, src in enumerate((feed, kill)):
            put_done(src.at[:, rows_of(row), :], coef_out.at[n, k], target)

    @pl.loop(0, 16)
    def _(i):
        row = first_row(i)
        put_done(initial.at[:, :, rows_of(row), :], first_out.at[i], place(x, row, group_there))

    @pl.loop(0, ENDS + SLOTS)
    def _(f):
        wait_on(land.at[f], halo_out.at[f])

    @pl.loop(0, SLOTS)
    def _(s):
        f = defect_field(s)

        @pl.when(has_halo(f))
        def _():
            wait_on(land.at[f], halo_out.at[f])

        @pl.when(jnp.logical_and(core == 0, f < DEFECT + 7))
        def _():
            wait_on(block_of(f), block_out.at[f])

        @pl.when(4 * group + s > 0)
        def _():
            residual_done(s)

    @pl.when(group < 3)
    def _():
        wait_on(back, back_out)

    @pl.when(chain)
    def _():
        wait_on(land.at[MIDDLE], halo_out.at[MIDDLE])

        @pl.when(late_half == 0)
        def _():
            wait_on(land.at[START], halo_out.at[LAST_PACK])
            wait_on(block_of(START), block_out.at[START])
            corrected_done(ENDS, 8, 0)

        @pl.when(late_half == 1)
        def _():
            corrected_done(steps[7], 7, first_turn + 7)

        for n in range(0, 7):
            corrected_done(steps[n], n, first_turn + n)

    wait_on(corrected, corr_in)

    @pl.when(tm > 0)
    def _():
        wait_on(residual, diff_in)

    @pl.when(tm == 0)
    def _():
        wait_on(residual.at[0], zero_sem)


def on_device(initial, estimate, feed_rate, kill_rate):
    dma = pltpu.SemaphoreType.DMA
    vmem = pltpu.VMEM
    both = pl.pallas_call(
        kernel,
        out_shape=jax.ShapeDtypeStruct((2,) + estimate.shape, F32),
        in_specs=[pl.BlockSpec(memory_space=pl.ANY)] * 4,
        out_specs=pl.BlockSpec(memory_space=pl.ANY),
        scratch_shapes=[
            vmem((FIELDS, 2, 16, 16, 128), F32),
            vmem((TRAIL, 5, 2, 4, 8, 128), F32),
            vmem((LAST_PACK + 1, 3, 2, 4, 8, 128), F32),
            vmem((2, 3, 16, 16, 128), F32),
            vmem((2, 2, 16, 16, 128), F32),
            vmem((SLOTS, 2, 8, 8, 128), F32),
            vmem((2, 8, 8, 128), F32),
            vmem((2, 8, 8, 128), F32),
            vmem((SLOTS + 1, 2, 8, 8, 128), F32),
            vmem((2, 2, 128, 128), F32),
            dma((TRAIL,)), dma((LAST_PACK + 1,)), dma((TRAIL,)), dma((TRAIL,)),
            dma((16,)), dma((4, 2)), dma((SLOTS, 4)), dma((9, 4)),
            dma, dma, dma, dma, dma, pltpu.SemaphoreType.REGULAR,
        ],
        compiler_params=pltpu.CompilerParams(
            collective_id=0, has_side_effects=True, vmem_limit_bytes=63 * 1024 * 1024
        ),
        name="mgrit_cycle",
    )(initial, estimate, feed_rate, kill_rate)
    return both[0], both[1]


def solution(mesh):
    placed = (
        P(None, "space", None, None),
        P("tm", None, "space", None, None),
        P("space", None, None),
        P("space", None, None),
    )
    return jax.shard_map(
        on_device,
        mesh=mesh,
        in_specs=placed,
        out_specs=(P("tm", None, "space", None, None), P("tm", None, "space", None, None)),
        check_vma=False,
    )
```

```python
import jax
import jax.numpy as jnp
from jax import lax
from jax.experimental import pallas as pl
from jax.experimental.pallas import tpu as pltpu
from jax.sharding import PartitionSpec as P

FACTOR = 4
time_step = 0.25
diffusion_substrate = 0.16
diffusion_catalyst = 0.08

MESH = pl.DeviceIdType.MESH
F32 = jnp.float32

STATE, COEF, ENDS, START, DEFECT, MIDDLE, TRAIL = 0, 4, 5, 9, 10, 17, 18
FIELDS = 24
SLOTS = 4
LAST_PACK = 18


def place(x, r, group):
    y = 2 * lax.div(group, 2) + lax.div(r, 8)
    z = jnp.where(r < 8, r, 15 - r)
    return y * 4 + lax.rem(z, 2) * 2 + 1 - lax.rem(group, 2), x * 4 + lax.div(z, 2)


def roll(value, by, axis):
    return pltpu.roll(value, by % value.shape[axis], axis)


def kernel(
    initial, estimate, feed, kill, both,
    field, land, pack, coef, work, late, coarse, back, diff, zero,
    halo_in, halo_out, block_in, block_out, first_out, coef_out, diff_out, corr_out,
    diff_in, corr_in, back_in, back_out, zero_sem, go,
):
    corrected, residual = both.at[0], both.at[1]
    tm = lax.axis_index("tm")
    space = lax.axis_index("space")
    x, z_hi = lax.div(space, 4), lax.rem(space, 4)
    y, z_lo, core = lax.div(tm, 4), lax.rem(lax.div(tm, 2), 2), lax.rem(tm, 2)
    z = 2 * z_hi + z_lo
    late_half = lax.div(y, 2)
    r = jnp.where(lax.rem(y, 2) == 0, z, 15 - z)
    group = 2 * late_half + 1 - core
    x_up, x_down = lax.rem(x + 1, 4), lax.rem(x + 3, 4)
    r_up, r_down = lax.rem(r + 1, 16), lax.rem(r + 15, 16)

    near = {}
    for dx, side in ((-1, x_down), (0, x), (1, x_up)):
        for dr, row in ((-1, r_down), (0, r), (1, r_up)):
            near[dx, dr] = place(side, row, 2 * late_half + 1)

    def neighbour(dx, dr, offset):
        base, part = near[dx, dr]
        return base + offset, part

    barrier = pltpu.get_barrier_semaphore()

    def is_me(target):
        return jnp.logical_and(target[0] == tm, target[1] == space)

    turn = lax.rem(tm + 1, 16)
    slot_there, group_there = lax.rem(turn, 4), lax.div(turn, 4)

    def greet(target):
        pl.semaphore_signal(barrier, inc=1, device_id=target, device_id_type=MESH)

    def greet_other(target):
        @pl.when(jnp.logical_not(is_me(target)))
        def _():
            greet(target)

    @pl.loop(0, 16)
    def _(i):
        greet_other((lax.rem(4 * group + lax.div(i, 4) + 15, 16), x * 4 + lax.rem(i, 4)))

    ahead = 2 * z_lo - 1
    for n in (1, -2, 3):
        there = lax.rem(z + n * ahead + 8, 8)
        greet((y * 4 + lax.rem(there, 2) * 2 + core, x * 4 + lax.div(there, 2)))

    for dx in (-1, 0, 1):
        for dr in (-1, 0, 1):
            if dx or dr:
                greet(neighbour(dx, dr, core))
    greet((tm + 1 - 2 * core, space))

    @pl.when(jnp.logical_and(late_half == 1, core == 1))
    def _():
        greet((tm - 8, space))
        greet((tm - 9, space))

    @pl.when(lax.rem(tm, 4) == 3)
    def _():
        @pl.loop(0, 16)
        def _(i):
            greet_other(place(x, i, lax.div(tm, 4)))

    mine_there = (group_there == group).astype(jnp.int32)
    mine_last = jnp.logical_and(lax.rem(tm, 4) == 3, lax.div(tm, 4) == group).astype(jnp.int32)
    pl.semaphore_wait(barrier, (16 - mine_there) + 3 + 8 + 1 + (1 - late_half) + (4 - mine_last))

    def put(src, dst, out_sem, in_sem, target):
        same = is_me(target)

        @pl.when(same)
        def _():
            pltpu.make_async_copy(src, dst, in_sem).start()

        @pl.when(jnp.logical_not(same))
        def _():
            pltpu.make_async_remote_copy(src, dst, out_sem, in_sem, device_id=target, device_id_type=MESH).start()

    def put_done(src, out_sem, target):
        @pl.when(jnp.logical_not(is_me(target)))
        def _():
            pltpu.make_async_copy(src, src, out_sem).wait()

    def rows_of(row):
        return pl.ds(pl.multiple_of(row * 8, 8), 8)

    here = pl.ds(4 + 2 * z_hi, 2)

    def coef_place(n):
        there = lax.rem(jnp.where(z_lo == 1, z + n, z + 8 - n), 8)
        row = jnp.where(lax.rem(y, 2) == 0, there, 15 - there)
        return row, (y * 4 + lax.rem(there, 2) * 2 + core, x * 4 + lax.div(there, 2))

    for n in range(4):
        row, target = coef_place(n)
        for k, src in enumerate((feed, kill)):
            put(src.at[:, rows_of(row), :], field.at[COEF, k, here, 0:8, :], coef_out.at[n, k], block_in.at[COEF], target)

    def first_row(i):
        n = lax.div(i, 2)
        step = jnp.where(lax.rem(n, 2) == 1, 4 - lax.div(n + 1, 2), 4 + lax.div(n, 2))
        there = lax.rem(z + step, 8)
        return jnp.where(lax.rem(i, 2) == 0, there, 15 - there)

    def first_put(src):
        @pl.loop(0, 16)
        def _(i):
            row = first_row(i)
            put(
                src.at[:, :, rows_of(row), :], field.at[slot_there, :, here, 0:8, :],
                first_out.at[i], block_in.at[slot_there], place(x, row, group_there),
            )

    @pl.when(tm < 15)
    def _():
        first_put(estimate.at[0])

    @pl.when(tm == 15)
    def _():
        first_put(initial)

    @pl.when(tm == 0)
    def _():
        zero[...] = jnp.zeros_like(zero)
        pltpu.make_async_copy(zero, residual.at[0], zero_sem).start()

    low = lax.broadcasted_iota(jnp.int32, (8, 128), 0)
    half = low < 4

    def block_of(f):
        return field.at[f, :, 4:12, 0:8, :]

    def send_halo(f, p, there, offset):
        for k in range(2):
            plane = [field[f, k, 4 + b, 0:8, :] for b in range(8)]
            for t in range(4):
                a, b = plane[2 * t], plane[2 * t + 1]
                pack[p, 0, k, t] = jnp.where(half, a, roll(b, 4, 0))
                pack[p, 1, k, t] = jnp.where(half, roll(a, 4, 0), b)
            for side, near in ((0, (7, 6, 5)), (1, (0, 1, 2))):
                a, b, c = (plane[n] for n in near)
                pack[p, 2, k, 2 * side] = jnp.where(low < 3, a, jnp.where(low < 5, roll(b, 3, 0), roll(c, 5, 0)))
                pack[p, 2, k, 2 * side + 1] = jnp.where(low >= 5, a, jnp.where(low >= 3, roll(b, 5, 0), roll(c, 3, 0)))

        def send(src, dst, dx, dr):
            pltpu.make_async_remote_copy(
                src, dst, halo_out.at[p], halo_in.at[there],
                device_id=neighbour(dx, dr, offset), device_id_type=MESH,
            ).start()

        send(pack.at[p, 2, :, 0], land.at[there, 4, :, 0], 1, -1)
        send(pack.at[p, 2, :, 1], land.at[there, 4, :, 1], 1, 1)
        send(pack.at[p, 2, :, 2], land.at[there, 4, :, 2], -1, -1)
        send(pack.at[p, 2, :, 3], land.at[there, 4, :, 3], -1, 1)
        send(field.at[f, :, 8:12, 0:8, :], land.at[there, 0], 1, 0)
        send(field.at[f, :, 4:8, 0:8, :], land.at[there, 1], -1, 0)
        send(pack.at[p, 0], land.at[there, 2], 0, -1)
        send(pack.at[p, 1], land.at[there, 3], 0, 1)

    def wait_on(ref, sem):
        pltpu.make_async_copy(ref, ref, sem).wait()

    def receive_halo(f):
        wait_on(land.at[f], halo_in.at[f])
        for k in range(2):
            for n in range(4):
                field[f, k, n, 0:8, :] = land[f, 0, k, n]
                field[f, k, 12 + n, 0:8, :] = land[f, 1, k, n]
            for t in range(4):
                a, b = land[f, 2, k, t], land[f, 3, k, t]
                field[f, k, 4 + 2 * t, 8:16, :] = jnp.where(half, a, roll(b, 4, 0))
                field[f, k, 5 + 2 * t, 8:16, :] = jnp.where(half, roll(a, 4, 0), b)
            for side, near in ((0, (3, 2, 1)), (1, (12, 13, 14))):
                a, b = land[f, 4, k, 2 * side], land[f, 4, k, 2 * side + 1]
                field[f, k, near[0], 8:16, :] = jnp.where(half, a, b)
                field[f, k, near[1], 8:16, :] = jnp.where(half, roll(a, 5, 0), roll(b, 3, 0))
                field[f, k, near[2], 8:16, :] = jnp.where(half, roll(a, 3, 0), roll(b, 5, 0))

    def sums(get, p, rows):
        result = []
        for k in range(2):
            m = get(k, p)
            c = m[:rows]
            s = get(k, p - 1)[:rows] + get(k, p + 1)[:rows]
            s = s + (roll(m, 1, 0)[:rows] + roll(m, -1, 0)[:rows])
            s = s + (roll(c, 1, 1) + roll(c, -1, 1))
            result.append((c, s))
        return result

    def update(middles, which, p, rows, h):
        (u, su), (v, sv) = middles
        reaction = (h * u) * (v * v) if h != 1.0 else u * (v * v)
        fa, fb, fc = (coef[which, n, p][:rows] for n in range(3))
        new_u = (fa * u + (h * diffusion_substrate) * su) + (fb - reaction)
        new_v = (fc * v + (h * diffusion_catalyst) * sv) + reaction
        return new_u, new_v

    def fine_step(get, store, lo, hi, whole):
        for p in range(lo, hi):
            rows = 16 if whole and lo < p < hi - 1 else 8
            new_u, new_v = update(sums(get, p, rows), 0, p, rows, time_step)
            store(0, p, rows, new_u)
            store(1, p, rows, new_v)

    def from_field(f):
        return lambda k, p: field[f, k, p]

    def from_work(w):
        return lambda k, p: work[w, k, p]

    def to_work(w):
        def store(k, p, rows, value):
            work[w, k, p, 0:rows, :] = value

        return store

    wait_on(block_of(COEF), block_in.at[COEF])
    send_halo(COEF, COEF, COEF, core)

    @pl.loop(0, SLOTS)
    def _(s):
        wait_on(block_of(s), block_in.at[s])
        send_halo(s, s, s, core)

    receive_halo(COEF)
    for which, h in ((0, time_step), (1, time_step * FACTOR)):
        for p in range(16):
            f, g = field[COEF, 0, p], field[COEF, 1, p]
            coef[which, 0, p] = (1.0 - 6.0 * h * diffusion_substrate) - h * f
            coef[which, 1, p] = h * f
            coef[which, 2, p] = (1.0 - 6.0 * h * diffusion_catalyst) - h * (f + g)

    @pl.loop(0, SLOTS)
    def _(s):
        receive_halo(s)
        fine_step(from_field(s), to_work(0), 1, 15, True)
        fine_step(from_work(0), to_work(1), 2, 14, True)
        fine_step(from_work(1), to_work(0), 3, 13, True)

        def store(k, p, rows, value):
            field[ENDS + s, k, p, 0:8, :] = value

        fine_step(from_work(0), store, 4, 12, False)
        send_halo(ENDS + s, ENDS + s, ENDS + s, core)

    my_rows = rows_of(r)

    def owner(turn_index, part):
        return turn_index, x * 4 + part

    def corrected_put(f, n, turn_index):
        for part in range(4):
            put(
                field.at[f, :, 4 + 2 * part : 6 + 2 * part, 0:8, :], corrected.at[0, :, :, my_rows, :],
                corr_out.at[n, part], corr_in, owner(turn_index, part),
            )

    def corrected_done(f, n, turn_index):
        for part in range(4):
            put_done(field.at[f, :, 4 + 2 * part : 6 + 2 * part, 0:8, :], corr_out.at[n, part], owner(turn_index, part))

    def residual_put(s):
        for part in range(4):
            put(
                diff.at[s, :, 2 * part : 2 * part + 2], residual.at[0, :, :, my_rows, :],
                diff_out.at[s, part], diff_in, owner(4 * group + s, part),
            )

    def residual_done(s):
        for part in range(4):
            put_done(diff.at[s, :, 2 * part : 2 * part + 2], diff_out.at[s, part], owner(4 * group + s, part))

    chain = core == 1
    chain_group = 2 * late_half

    def defect_field(s):
        return jnp.where(late_half == 0, START, DEFECT - 8) + 4 * group + s

    def has_halo(f):
        return jnp.logical_and(f != DEFECT + 3, f < DEFECT + 6)

    @pl.when(group == 0)
    def _():
        corrected_put(ENDS, 8, 0)

    @pl.loop(0, SLOTS)
    def _(s):
        f = defect_field(s)
        receive_halo(ENDS + s)
        for p in range(1, 15):
            rows = 16 if 1 < p < 14 else 8
            middles = sums(from_field(ENDS + s), p, rows)
            new_u, new_v = update(middles, 0, p, rows, time_step)
            work[0, 0, p, 0:rows, :] = new_u
            work[0, 1, p, 0:rows, :] = new_v
            if 4 <= p < 12:
                new_u, new_v = update([(c[:8], w[:8]) for c, w in middles], 1, p, 8, time_step * FACTOR)
                coarse[0, p - 4] = new_u
                coarse[1, p - 4] = new_v
        fine_step(from_work(0), to_work(1), 2, 14, True)
        fine_step(from_work(1), to_work(0), 3, 13, True)
        opening = jnp.logical_and(group == 0, s == 0)
        following = jnp.minimum(s + 1, SLOTS - 1)

        def store(k, p, rows, value):
            late[s, k, p - 4] = value
            field[f, k, p, 0:8, :] = value - jnp.where(opening, 0.0, coarse[k, p - 4])
            diff[s + 1, k, p - 4] = value - field[ENDS + following, k, p, 0:8, :]

        fine_step(from_work(0), store, 4, 12, False)

        @pl.when(has_halo(f))
        def _():
            send_halo(f, f, f, 1)

        @pl.when(jnp.logical_and(core == 0, f < DEFECT + 7))
        def _():
            pltpu.make_async_remote_copy(
                block_of(f), block_of(f), block_out.at[f], block_in.at[f],
                device_id=place(x, r, chain_group), device_id_type=MESH,
            ).start()

        @pl.when(jnp.logical_and(s < SLOTS - 1, late_half == 1))
        def _():
            residual_put(s + 1)

        @pl.when(jnp.logical_and(s == SLOTS - 1, group < 3))
        def _():
            pltpu.make_async_remote_copy(
                late.at[s], back, back_out, back_in, device_id=place(x, r, group + 1), device_id_type=MESH
            ).start()

    def coarse_step(src, dst, d, lo, hi, whole):
        for p in range(lo, hi):
            rows = 16 if whole and lo < p < hi - 1 else 8
            new_u, new_v = update(sums(from_field(src), p, rows), 1, p, rows, time_step * FACTOR)
            field[dst, 0, p, 0:rows, :] = new_u + field[d, 0, p, 0:rows, :]
            field[dst, 1, p, 0:rows, :] = new_v + field[d, 1, p, 0:rows, :]

    steps = (START, TRAIL, TRAIL + 1, TRAIL + 2, MIDDLE, TRAIL + 3, TRAIL + 4, TRAIL + 5)
    first_turn = jnp.where(late_half == 0, 1, 8)

    def first_residual():
        wait_on(back, back_in)
        for k in range(2):
            for b in range(8):
                diff[0, k, b] = back[k, b] - field[ENDS, k, 4 + b, 0:8, :]
        residual_put(0)

    @pl.when(chain)
    def _():
        @pl.when(late_half == 1)
        def _():
            first_residual()

        for n in range(3):
            receive_halo(DEFECT + n)
        receive_halo(START)

        @pl.when(late_half == 1)
        def _():
            wait_on(block_of(START), block_in.at[START])
            corrected_put(START, 0, 8)

        coarse_step(steps[0], steps[1], DEFECT, 1, 15, True)
        coarse_step(steps[1], steps[2], DEFECT + 1, 2, 14, True)
        coarse_step(steps[2], steps[3], DEFECT + 2, 3, 13, True)

        @pl.when(late_half == 0)
        def _():
            wait_on(block_of(DEFECT + 3), block_in.at[DEFECT + 3])

        coarse_step(steps[3], steps[4], DEFECT + 3, 4, 12, False)
        send_halo(MIDDLE, MIDDLE, MIDDLE, core)

        for n in range(4, 7):
            wait_on(block_of(DEFECT + n), block_in.at[DEFECT + n])

        @pl.when(late_half == 1)
        def _():
            for n in range(1, 5):
                corrected_put(steps[n], n, first_turn + n)

        for n in range(4, 6):
            receive_halo(DEFECT + n)
        receive_halo(MIDDLE)
        coarse_step(steps[4], steps[5], DEFECT + 4, 2, 14, True)

        @pl.when(late_half == 1)
        def _():
            corrected_put(steps[5], 5, first_turn + 5)

        coarse_step(steps[5], steps[6], DEFECT + 5, 3, 13, True)

        @pl.when(late_half == 1)
        def _():
            corrected_put(steps[6], 6, first_turn + 6)

        coarse_step(steps[6], steps[7], DEFECT + 6, 4, 12, False)

        @pl.when(late_half == 0)
        def _():
            send_halo(steps[7], LAST_PACK, START, 9)
            pltpu.make_async_remote_copy(
                block_of(steps[7]), block_of(START), block_out.at[START], block_in.at[START],
                device_id=place(x, r, 2), device_id_type=MESH,
            ).start()
            pl.semaphore_signal(go, inc=1, device_id=(tm - 1, space), device_id_type=MESH)
            for n in range(0, 7):
                corrected_put(steps[n], n, first_turn + n)

        @pl.when(late_half == 1)
        def _():
            corrected_put(steps[7], 7, first_turn + 7)

        @pl.when(late_half == 0)
        def _():
            for n in range(1, SLOTS):
                residual_put(n)

    @pl.when(jnp.logical_and(core == 0, late_half == 0))
    def _():
        pl.semaphore_wait(go, 1)
        for n in range(1, SLOTS):
            residual_put(n)

    @pl.when(core == 0)
    def _():
        first_residual()

    for n in range(4):
        row, target = coef_place(n)
        for k, src in enumerate((feed, kill)):
            put_done(src.at[:, rows_of(row), :], coef_out.at[n, k], target)

    @pl.loop(0, 16)
    def _(i):
        row = first_row(i)
        put_done(initial.at[:, :, rows_of(row), :], first_out.at[i], place(x, row, group_there))

    @pl.loop(0, ENDS + SLOTS)
    def _(f):
        wait_on(land.at[f], halo_out.at[f])

    @pl.loop(0, SLOTS)
    def _(s):
        f = defect_field(s)

        @pl.when(has_halo(f))
        def _():
            wait_on(land.at[f], halo_out.at[f])

        @pl.when(jnp.logical_and(core == 0, f < DEFECT + 7))
        def _():
            wait_on(block_of(f), block_out.at[f])

        @pl.when(4 * group + s > 0)
        def _():
            residual_done(s)

    @pl.when(group < 3)
    def _():
        wait_on(back, back_out)

    @pl.when(chain)
    def _():
        wait_on(land.at[MIDDLE], halo_out.at[MIDDLE])

        @pl.when(late_half == 0)
        def _():
            wait_on(land.at[START], halo_out.at[LAST_PACK])
            wait_on(block_of(START), block_out.at[START])
            corrected_done(ENDS, 8, 0)

        @pl.when(late_half == 1)
        def _():
            corrected_done(steps[7], 7, first_turn + 7)

        for n in range(0, 7):
            corrected_done(steps[n], n, first_turn + n)

    wait_on(corrected, corr_in)

    @pl.when(tm > 0)
    def _():
        wait_on(residual, diff_in)

    @pl.when(tm == 0)
    def _():
        wait_on(residual.at[0], zero_sem)


def on_device(initial, estimate, feed_rate, kill_rate):
    dma = pltpu.SemaphoreType.DMA
    vmem = pltpu.VMEM
    both = pl.pallas_call(
        kernel,
        out_shape=jax.ShapeDtypeStruct((2,) + estimate.shape, F32),
        in_specs=[pl.BlockSpec(memory_space=pl.ANY)] * 4,
        out_specs=pl.BlockSpec(memory_space=pl.ANY),
        scratch_shapes=[
            vmem((FIELDS, 2, 16, 16, 128), F32),
            vmem((TRAIL, 5, 2, 4, 8, 128), F32),
            vmem((LAST_PACK + 1, 3, 2, 4, 8, 128), F32),
            vmem((2, 3, 16, 16, 128), F32),
            vmem((2, 2, 16, 16, 128), F32),
            vmem((SLOTS, 2, 8, 8, 128), F32),
            vmem((2, 8, 8, 128), F32),
            vmem((2, 8, 8, 128), F32),
            vmem((SLOTS + 1, 2, 8, 8, 128), F32),
            vmem((2, 2, 128, 128), F32),
            dma((TRAIL,)), dma((LAST_PACK + 1,)), dma((TRAIL,)), dma((TRAIL,)),
            dma((16,)), dma((4, 2)), dma((SLOTS, 4)), dma((9, 4)),
            dma, dma, dma, dma, dma, pltpu.SemaphoreType.REGULAR,
        ],
        compiler_params=pltpu.CompilerParams(
            collective_id=0, has_side_effects=True, vmem_limit_bytes=63 * 1024 * 1024
        ),
        name="mgrit_cycle",
    )(initial, estimate, feed_rate, kill_rate)
    return both[0], both[1]


def solution(mesh):
    placed = (
        P(None, "space", None, None),
        P("tm", None, "space", None, None),
        P("space", None, None),
        P("space", None, None),
    )
    return jax.shard_map(
        on_device,
        mesh=mesh,
        in_specs=placed,
        out_specs=(P("tm", None, "space", None, None), P("tm", None, "space", None, None)),
        check_vma=False,
    )
```
